256 devices in a mesh: row: 16 (over y_lo, z), col: 16 (over x, y_hi, core).
Axes of the slice: x: 4, y: 4 (y_hi: 2, y_lo: 2; y = y_hi * 2 + y_lo), z: 8, core: 2. Of those that a mesh axis runs over, the one named last changes fastest.
Arguments:
- pair: bfloat16 [992, 992, 128], P('row', 'col'), may hold values from -6 to 6
- pair_mask: int32 [992, 992], P('row', 'col'), may hold values 0 or 1
- norm_in_gain: float32 [128], replicated, may hold values from 0.1 to 1.9
- proj_weight: bfloat16 [128, 512], replicated, may hold values from -0.5 to 0.5
- gate_weight: bfloat16 [128, 128], replicated, may hold values from -0.5 to 0.5
- norm_mid_gain: float32 [128], replicated, may hold values from 0.1 to 1.9
- out_weight: bfloat16 [128, 128], replicated, may hold values from -0.5 to 0.5
- norm_tr_gain: float32 [128], replicated, may hold values from 0.1 to 1.9
- tr_in_weight: bfloat16 [128, 1024], replicated, may hold values from -0.5 to 0.5
- tr_out_weight: bfloat16 [512, 128], replicated, may hold values from -0.25 to 0.25
Outputs:
- new_pair: bfloat16 [992, 992, 128], P('row', 'col')
The draws below stay inside these ranges and needn't reach their ends.
All inputs are finite; a program needn't handle non-finite values. No bound on the sum of `pair_mask` on one device may be relied on, other than what follows from the above.
Results may differ from the reference program's by a relative error of at most 0.02.
Values may be sent and summed in bfloat16 or wider, within the bound.
No kernel may reach another device: no remote copies, remote signals or barrier semaphores. Data moves between devices by JAX's collectives and lax.ppermute only.
A program may use at most 192 MiB of HBM per device.

```python
import jax
import jax.numpy as jnp
from jax import lax

C = 128
CH = 128
FT = 512
N = 992
COLS_DEV = 62


def set_ends(drawn, own_key, least, largest):
    extent = drawn.shape
    place = [jax.random.randint(jax.random.fold_in(own_key, axis), (), 0, extent[axis]) for axis in range(len(extent))]
    drawn = drawn.at[tuple(place)].set(least)
    longest = extent.index(max(extent))
    place[longest] = (place[longest] + 1) % extent[longest]
    return drawn.at[tuple(place)].set(largest)


def steps_of(rng, dims, split, low, top_value):
    def one(dim, blocks):
        draws = jax.random.uniform(jax.random.fold_in(jax.random.fold_in(rng, 6), dim), (blocks,), jnp.float32, low / len(split), top_value / len(split))
        return jnp.repeat(jnp.exp(draws), dims[dim] // blocks).reshape((-1,) + (1,) * (len(dims) - dim - 1))

    level = one(*split[0])
    for cut in split[1:]:
        level = level * one(*cut)
    return level


def scatter_about(own_key, dims, spread, limit, cuts=(), kind=jnp.bfloat16):
    factor_of = steps_of(own_key, dims, cuts, -0.22, 0.18) if cuts else 1.0
    result = jax.random.normal(own_key, dims, jnp.float32) * spread * factor_of
    return jnp.minimum(jnp.maximum(result, -limit), limit).astype(kind)


def setup_inputs(seed: int = 0) -> dict:
    seeds = jax.random.split(jax.random.key(seed), 11)
    pair = scatter_about(seeds[0], (N, N, C), 1.0, 6.0, ((0, 16), (1, 16)))
    pair_mask = set_ends((jax.random.randint(seeds[1], (N, N), 0, 10) < 9).astype(jnp.int32), jax.random.fold_in(seeds[1], 1), 0, 1)
    norm_in_gain = jnp.clip(1.0 + 0.18 * jax.random.normal(seeds[2], (C,), jnp.float32), 0.1, 1.9)
    proj_weight = scatter_about(seeds[3], (C, 4 * CH), C ** -0.5, 0.5)
    gate_weight = scatter_about(seeds[4], (C, C), C ** -0.5, 0.5)
    norm_mid_gain = jnp.clip(1.0 + 0.18 * jax.random.normal(seeds[5], (CH,), jnp.float32), 0.1, 1.9)
    out_weight = scatter_about(seeds[6], (CH, C), CH ** -0.5, 0.5)
    norm_tr_gain = jnp.clip(1.0 + 0.18 * jax.random.normal(seeds[7], (C,), jnp.float32), 0.1, 1.9)
    tr_in_weight = scatter_about(seeds[8], (C, 2 * FT), C ** -0.5, 0.5)
    tr_out_weight = scatter_about(seeds[9], (FT, C), FT ** -0.5, 0.25)
    return dict(pair=pair, pair_mask=pair_mask, norm_in_gain=norm_in_gain, proj_weight=proj_weight, gate_weight=gate_weight, norm_mid_gain=norm_mid_gain, out_weight=out_weight, norm_tr_gain=norm_tr_gain, tr_in_weight=tr_in_weight, tr_out_weight=tr_out_weight)


def layer_norm(values, norm_gain):
    average = lax.optimization_barrier(jnp.mean(values, axis=-1, keepdims=True))
    centered = values - average
    variance = lax.optimization_barrier(jnp.mean(centered * centered, axis=-1, keepdims=True))
    return centered * lax.rsqrt(variance + 1e-05) * norm_gain

def gated_half(normed, keep_mask, weight_part, hidden_width):
    projected = jnp.dot(normed, weight_part, preferred_element_type=jnp.float32)
    gated = keep_mask * jax.nn.sigmoid(projected[:, :hidden_width]) * projected[:, hidden_width:]
    return gated.astype(jnp.bfloat16)

def finish(pair_rows, normed, combined, gate_weight, norm_mid_gain, out_weight, norm_tr_gain, tr_in_weight, tr_out_weight):
    residual_in = pair_rows.astype(jnp.float32)
    gate_value = jax.nn.sigmoid(jnp.dot(normed, gate_weight, preferred_element_type=jnp.float32))
    mixed_norm = layer_norm(combined, norm_mid_gain).astype(jnp.bfloat16)
    update = gate_value * jnp.dot(mixed_norm, out_weight, preferred_element_type=jnp.float32)
    middle = lax.optimization_barrier((residual_in + update).astype(jnp.bfloat16))
    middle_wide = middle.astype(jnp.float32)
    tr_normed = layer_norm(middle_wide, norm_tr_gain).astype(jnp.bfloat16)
    tr_width = tr_out_weight.shape[0]
    hidden = jnp.dot(tr_normed, tr_in_weight, preferred_element_type=jnp.float32)
    activated = (jax.nn.silu(hidden[:, :tr_width]) * hidden[:, tr_width:]).astype(jnp.bfloat16)
    return (middle_wide + jnp.dot(activated, tr_out_weight, preferred_element_type=jnp.float32)).astype(jnp.bfloat16)

def reference(pair, pair_mask, norm_in_gain, proj_weight, gate_weight, norm_mid_gain, out_weight, norm_tr_gain, tr_in_weight, tr_out_weight):

    def front(inputs):
        pair_rows, mask_rows = inputs
        normed = layer_norm(pair_rows.astype(jnp.float32), norm_in_gain).astype(jnp.bfloat16)
        keep_mask = mask_rows.astype(jnp.float32)[:, None]
        left_gated = gated_half(normed, keep_mask, proj_weight[:, :2 * CH], CH)
        right_gated = gated_half(normed, keep_mask, proj_weight[:, 2 * CH:], CH)
        return (left_gated, right_gated)
    left_all, right_all = lax.map(front, (pair, pair_mask))
    left_first = jnp.transpose(left_all, (2, 0, 1))
    right_first = jnp.transpose(right_all, (2, 0, 1))

    def accumulate(running, block_index):
        begin_col = (block_index * COLS_DEV).astype(jnp.int32)
        left_block = lax.dynamic_slice_in_dim(left_first, begin_col, COLS_DEV, 2).astype(jnp.float32)
        right_block = lax.dynamic_slice_in_dim(right_first, begin_col, COLS_DEV, 2).astype(jnp.float32)
        block_sum = jnp.einsum('cik,cjk->cij', left_block, right_block)
        block_sum = lax.optimization_barrier(block_sum.astype(jnp.bfloat16)).astype(jnp.float32)
        return (running + block_sum, None)
    combined, _ = lax.scan(accumulate, jnp.zeros((CH, N, N), jnp.float32), jnp.arange(N // COLS_DEV, dtype=jnp.int32))
    combined = jnp.transpose(combined, (1, 2, 0))

    def back(inputs):
        pair_rows, combined_rows = inputs
        normed = layer_norm(pair_rows.astype(jnp.float32), norm_in_gain).astype(jnp.bfloat16)
        return finish(pair_rows, normed, combined_rows, gate_weight, norm_mid_gain, out_weight, norm_tr_gain, tr_in_weight, tr_out_weight)
    return lax.map(back, (pair, combined))
```

```python
import functools

import jax
import jax.numpy as jnp
from jax import lax
from jax.experimental import pallas as pl
from jax.experimental.pallas import tpu as pltpu
from jax.sharding import Mesh
from jax.sharding import PartitionSpec as P

SIDE = 64
LINES = 32
LANES = 128
VMEM_LIMIT = 48 * 1024 * 1024
F32 = jnp.float32
BF16 = jnp.bfloat16


def norm_rows(values, gain):
    average = jnp.mean(values, axis=-1, keepdims=True)
    centered = values - average
    variance = jnp.mean(centered * centered, axis=-1, keepdims=True)
    return centered * lax.rsqrt(variance + 1e-05) * gain


def swap_halves(values):
    return pltpu.roll(values, LANES // 2, axis=1)


def low_half(rows):
    return lax.broadcasted_iota(jnp.int32, (rows, LANES), 1) < LANES // 2


def project_kernel(side, step, pair_ref, mask_ref, gain_ref, weight_ref, out_ref, rows, mask, weight, lines):
    channels = pair_ref.shape[-1]
    rows[...] = jnp.zeros_like(rows)
    mask[...] = jnp.zeros_like(mask)
    mask[0:side, 0:side] = mask_ref[...].astype(F32)
    mask[0:LINES, :] = jnp.where(low_half(LINES), mask[0:LINES, :], swap_halves(mask[LINES:, :]))
    weight[...] = weight_ref[...].astype(F32).T.astype(BF16)
    gain = gain_ref[...]

    def body(group, _):
        for u in range(step):
            line = group * step + u
            for half in range(2):
                i = line if half == 0 else jnp.minimum(LINES + line, side - 1)
                start = (2 * u + half) * SIDE
                rows[start : start + side, :] = norm_rows(pair_ref[i].astype(F32), gain)
        projected = lax.dot_general(
            weight[...], rows[...].astype(BF16), (((1,), (1,)), ((), ())), preferred_element_type=F32
        )
        for u in range(step):
            line = group * step + u
            part = projected[:, u * LANES : (u + 1) * LANES]
            keep = mask[pl.ds(line, 1), :]
            for which in range(2):
                at = 2 * which * channels
                gate, value = part[at : at + channels], part[at + channels : at + 2 * channels]
                lines[:, which * LINES + line, :] = keep * jax.nn.sigmoid(gate) * value
        return 0

    lax.fori_loop(0, LINES // step, body, 0)
    out_ref[...] = lines[...].astype(BF16)


def project(pair, pair_mask, gain, weight):
    side, _, channels = pair.shape
    step = 4
    return pl.pallas_call(
        functools.partial(project_kernel, side, step),
        out_shape=jax.ShapeDtypeStruct((channels, 2 * LINES, LANES), BF16),
        scratch_shapes=[
            pltpu.VMEM((step * LANES, channels), F32),
            pltpu.VMEM((SIDE, LANES), F32),
            pltpu.VMEM((weight.shape[1], channels), BF16),
            pltpu.VMEM((channels, 2 * LINES, LANES), F32),
        ],
        compiler_params=pltpu.CompilerParams(vmem_limit_bytes=VMEM_LIMIT),
    )(pair, pair_mask, gain.reshape(1, -1), weight)


def multiply_kernel(blocks, chips, core_ref, in_ref, keep_ref, give_ref, left, right, product):
    core = core_ref[0]
    pairs = chips // 2
    low = low_half(LINES)

    def arrange(r, _):
        for which, target in enumerate((left, right)):
            for m in range(pairs):
                first = in_ref[r * chips + 2 * m, which * LINES : (which + 1) * LINES, :].astype(F32)
                second = in_ref[r * chips + 2 * m + 1, which * LINES : (which + 1) * LINES, :].astype(F32)
                columns = slice(m * LANES, (m + 1) * LANES)
                target[pl.ds(r * SIDE, LINES), columns] = jnp.where(low, first, swap_halves(second)).astype(BF16)
                target[pl.ds(r * SIDE + LINES, LINES), columns] = jnp.where(
                    low, swap_halves(first), second
                ).astype(BF16)
        return 0

    lax.fori_loop(0, blocks, arrange, 0)
    width = product.shape[1]
    groups = blocks * SIDE // width
    per_group = width // LANES
    for group in range(groups):
        product[...] = lax.dot_general(
            left[...],
            right[group * width : (group + 1) * width, :],
            (((1,), (1,)), ((), ())),
            preferred_element_type=F32,
        )

        def deliver(r, _):
            for m in range(per_group):
                columns = slice(m * LANES, (m + 1) * LANES)
                first = product[pl.ds(r * SIDE, LINES), columns]
                second = product[pl.ds(r * SIDE + LINES, LINES), columns]
                even = jnp.where(low, first, swap_halves(second))
                odd = jnp.where(low, swap_halves(first), second)
                piece = r * chips + group * per_group + m
                keep_ref[piece] = jnp.where(core == 0, even, odd).astype(BF16)
                give_ref[piece] = jnp.where(core == 0, odd, even).astype(BF16)
            return 0

        lax.fori_loop(0, blocks, deliver, 0)


def multiply(received, core, blocks, chips):
    depth = chips * SIDE
    shape = jax.ShapeDtypeStruct((blocks * chips, LINES, LANES), BF16)
    return pl.pallas_call(
        functools.partial(multiply_kernel, blocks, chips),
        out_shape=(shape, shape),
        in_specs=[pl.BlockSpec(memory_space=pltpu.SMEM), pl.BlockSpec(memory_space=pltpu.VMEM)],
        scratch_shapes=[
            pltpu.VMEM((blocks * SIDE, depth), BF16),
            pltpu.VMEM((blocks * SIDE, depth), BF16),
            pltpu.VMEM((blocks * SIDE, 256), F32),
        ],
        compiler_params=pltpu.CompilerParams(vmem_limit_bytes=VMEM_LIMIT),
    )(core, received)


def finish_kernel(
    side,
    step,
    pair_ref,
    in_ref,
    norm_in_ref,
    gate_ref,
    norm_mid_ref,
    out_weight_ref,
    norm_tr_ref,
    tr_in_ref,
    tr_out_ref,
    out_ref,
    rows,
    lines,
    result,
):
    hidden_width = tr_out_ref.shape[0]
    rows[...] = jnp.zeros_like(rows)
    lines[...] = in_ref[...].astype(F32)

    def body(group, _):
        mixed = []
        for u in range(step):
            line = group * step + u
            for half in range(2):
                i = line if half == 0 else jnp.minimum(LINES + line, side - 1)
                start = (2 * u + half) * SIDE
                rows[start : start + side, :] = pair_ref[i].astype(F32)
            combined = lines[:, line, :]
            average = jnp.mean(combined, axis=0, keepdims=True)
            centered = combined - average
            variance = jnp.mean(centered * centered, axis=0, keepdims=True)
            mixed.append((centered * lax.rsqrt(variance + 1e-05)).T)
        mixed_norm = (jnp.concatenate(mixed, axis=0) * norm_mid_ref[...]).astype(BF16)
        residual = rows[...]
        normed = norm_rows(residual, norm_in_ref[...]).astype(BF16)
        gate = jax.nn.sigmoid(jnp.dot(normed, gate_ref[...], preferred_element_type=F32))
        update = gate * jnp.dot(mixed_norm, out_weight_ref[...], preferred_element_type=F32)
        middle = (residual + update).astype(BF16).astype(F32)
        tr_normed = norm_rows(middle, norm_tr_ref[...]).astype(BF16)
        hidden = jnp.dot(tr_normed, tr_in_ref[...], preferred_element_type=F32)
        activated = (jax.nn.silu(hidden[:, :hidden_width]) * hidden[:, hidden_width:]).astype(BF16)
        result[...] = middle + jnp.dot(activated, tr_out_ref[...], preferred_element_type=F32)
        for u in range(step):
            line = group * step + u
            start = 2 * u * SIDE
            out_ref[line] = result[start : start + side, :].astype(BF16)

            @pl.when(LINES + line < side)
            def _():
                out_ref[LINES + line] = result[start + SIDE : start + SIDE + side, :].astype(BF16)

        return 0

    lax.fori_loop(0, LINES // step, body, 0)


def finish(pair, received, norm_in_gain, gate_weight, norm_mid_gain, out_weight, norm_tr_gain, tr_in_weight, tr_out_weight):
    side, _, channels = pair.shape
    step = 4
    return pl.pallas_call(
        functools.partial(finish_kernel, side, step),
        out_shape=jax.ShapeDtypeStruct(pair.shape, BF16),
        scratch_shapes=[
            pltpu.VMEM((step * LANES, channels), F32),
            pltpu.VMEM(received.shape, F32),
            pltpu.VMEM((step * LANES, channels), F32),
        ],
        compiler_params=pltpu.CompilerParams(vmem_limit_bytes=VMEM_LIMIT),
    )(
        pair,
        received,
        norm_in_gain.reshape(1, -1),
        gate_weight,
        norm_mid_gain.reshape(1, -1),
        out_weight,
        norm_tr_gain.reshape(1, -1),
        tr_in_weight,
        tr_out_weight,
    )


def local(
    blocks,
    chips,
    pair,
    pair_mask,
    norm_in_gain,
    proj_weight,
    gate_weight,
    norm_mid_gain,
    out_weight,
    norm_tr_gain,
    tr_in_weight,
    tr_out_weight,
):
    every_chip = ("row", "chip")
    sent = project(pair, pair_mask, norm_in_gain, proj_weight)
    received = lax.all_to_all(sent, every_chip, 0, 0, tiled=True)
    core = lax.axis_index("core").astype(jnp.int32).reshape(1)
    keep, give = multiply(received, core, blocks, chips)
    other = lax.ppermute(give, "core", [(0, 1), (1, 0)])
    combined = (keep.astype(F32) + other.astype(F32)).astype(BF16)
    returned = lax.all_to_all(combined, every_chip, 0, 0, tiled=True)
    return finish(
        pair, returned, norm_in_gain, gate_weight, norm_mid_gain, out_weight, norm_tr_gain, tr_in_weight, tr_out_weight
    )


def solution(mesh):
    blocks, columns = mesh.devices.shape
    chips = columns // 2
    split = Mesh(mesh.devices.reshape(blocks, chips, 2), ("row", "chip", "core"))
    in_specs = (P("row", ("chip", "core"), None), P("row", ("chip", "core"))) + (P(),) * 8
    out_specs = P("row", ("chip", "core"), None)
    return jax.shard_map(
        functools.partial(local, blocks, chips), mesh=split, in_specs=in_specs, out_specs=out_specs, check_vma=False
    )
```

```python
import functools

import jax
import jax.numpy as jnp
from jax import lax
from jax.experimental import pallas as pl
from jax.experimental.pallas import tpu as pltpu
from jax.sharding import Mesh
from jax.sharding import PartitionSpec as P

SIDE = 64
LINES = 32
LANES = 128
VMEM_LIMIT = 48 * 1024 * 1024
F32 = jnp.float32
BF16 = jnp.bfloat16


def norm_rows(values, gain):
    channels = values.shape[-1]
    weight = jnp.full((channels, channels), 1.0 / channels, BF16)
    centered = values.astype(F32) - jnp.dot(values, weight, preferred_element_type=F32)
    variance = jnp.mean(centered * centered, axis=-1, keepdims=True)
    return (centered * lax.rsqrt(variance + 1e-05) * gain).astype(BF16)


def swap_halves(values):
    return pltpu.roll(values, LANES // 2, axis=1)


def low_half(rows):
    return lax.broadcasted_iota(jnp.int32, (rows, LANES), 1) < LANES // 2


def project_kernel(
    side,
    step,
    pair_hbm,
    mask_hbm,
    gain_hbm,
    weight_hbm,
    out_hbm,
    pair_ref,
    mask_ref,
    gain_ref,
    weight_ref,
    mask,
    rows,
    out_ref,
    sems,
    out_sems,
):
    channels = pair_ref.shape[-1]
    groups = LINES // step
    small = [
        pltpu.make_async_copy(source, target, sems.at[n])
        for n, (source, target) in enumerate(((mask_hbm, mask_ref), (weight_hbm, weight_ref), (gain_hbm, gain_ref)))
    ]
    parts = []
    for group in range(groups):
        for half in range(2):
            first = half * LINES + group * step
            span = pl.ds(first, min(step, side - first))
            parts.append(pltpu.make_async_copy(pair_hbm.at[span], pair_ref.at[span], sems.at[3 + len(parts)]))
    outgoing = []
    for copy in small + parts:
        copy.start()
    rows[...] = jnp.zeros_like(rows)
    mask[...] = jnp.zeros_like(mask)
    for copy in small:
        copy.wait()
    mask[0:side, 0:side] = mask_ref[...].astype(F32)
    low = low_half(LINES)
    keep = jnp.where(low, mask[0:LINES, :], swap_halves(mask[LINES:, :]))
    weight = weight_ref[...].astype(F32).T.astype(BF16)
    for group in range(groups):
        parts[2 * group].wait()
        parts[2 * group + 1].wait()
        for u in range(step):
            for half in range(2):
                i = half * LINES + group * step + u
                if i < side:
                    start = (2 * u + half) * SIDE
                    rows[start : start + side, :] = pair_ref[i]
        projected = lax.dot_general(
            weight, norm_rows(rows[...], gain_ref[...]), (((1,), (1,)), ((), ())), preferred_element_type=F32
        )
        for which in range(2):
            made = []
            for u in range(step):
                part = projected[:, u * LANES : (u + 1) * LANES]
                at = 2 * which * channels
                gate, value = part[at : at + channels], part[at + channels : at + 2 * channels]
                line = group * step + u
                made.append(keep[line : line + 1, :] * jax.nn.sigmoid(gate) * value)
            first = which * LINES + group * step
            span = pl.ds(first, step)
            out_ref[:, span, :] = pltpu.einshape("tcl->ctl", jnp.stack(made)).astype(BF16)
            copy = pltpu.make_async_copy(out_ref.at[:, span], out_hbm.at[:, span], out_sems.at[len(outgoing)])
            copy.start()
            outgoing.append(copy)
    for copy in outgoing:
        copy.wait()


def project(pair, pair_mask, gain, weight):
    side, _, channels = pair.shape
    step = 16
    return pl.pallas_call(
        functools.partial(project_kernel, side, step),
        out_shape=jax.ShapeDtypeStruct((channels, 2 * LINES, LANES), BF16),
        in_specs=[pl.BlockSpec(memory_space=pltpu.HBM)] * 4,
        out_specs=pl.BlockSpec(memory_space=pltpu.HBM),
        scratch_shapes=[
            pltpu.VMEM(pair.shape, BF16),
            pltpu.VMEM(pair_mask.shape, jnp.int32),
            pltpu.VMEM((1, channels), F32),
            pltpu.VMEM(weight.shape, BF16),
            pltpu.VMEM((SIDE, LANES), F32),
            pltpu.VMEM((step * LANES, channels), BF16),
            pltpu.VMEM((channels, 2 * LINES, LANES), BF16),
            pltpu.SemaphoreType.DMA((3 + 2 * LINES // step,)),
            pltpu.SemaphoreType.DMA((2 * LINES // step,)),
        ],
        compiler_params=pltpu.CompilerParams(vmem_limit_bytes=62 * 1024 * 1024),
    )(pair, pair_mask, gain.reshape(1, -1), weight)


def multiply_kernel(blocks, chips, parity_ref, in_ref, out_ref, left, right):
    parity = parity_ref[0]
    low = low_half(LINES)

    def arrange_left(r, _):
        for m in range(chips):
            left[pl.ds(r * LINES, LINES), m * LANES : (m + 1) * LANES] = in_ref[r * chips + m, 0:LINES, :]
        return 0

    def arrange_right(s, _):
        for m in range(chips):
            piece = in_ref[(2 * s + parity) * chips + m, LINES : 2 * LINES, :].astype(F32)
            swapped = swap_halves(piece)
            columns = slice(m * LANES, (m + 1) * LANES)
            for n, values in enumerate(
                (
                    jnp.where(low, piece, 0.0),
                    jnp.where(low, swapped, 0.0),
                    jnp.where(low, 0.0, swapped),
                    jnp.where(low, 0.0, piece),
                )
            ):
                right[pl.ds(s * LANES + n * LINES, LINES), columns] = values.astype(BF16)
        return 0

    lax.fori_loop(0, blocks, arrange_left, 0)
    lax.fori_loop(0, blocks // 2, arrange_right, 0)
    width = 2 * LANES
    for group in range(blocks // 4):
        product = lax.dot_general(
            left[...],
            right[group * width : (group + 1) * width, :],
            (((1,), (1,)), ((), ())),
            preferred_element_type=F32,
        ).astype(BF16)
        for r in range(blocks):
            for n in range(2):
                out_ref[r * chips + 2 * group + n] = product[
                    r * LINES : (r + 1) * LINES, n * LANES : (n + 1) * LANES
                ]


def multiply(received, parity, blocks, chips):
    return pl.pallas_call(
        functools.partial(multiply_kernel, blocks, chips),
        out_shape=jax.ShapeDtypeStruct((blocks * chips, LINES, LANES), BF16),
        in_specs=[pl.BlockSpec(memory_space=pltpu.SMEM), pl.BlockSpec(memory_space=pltpu.VMEM)],
        scratch_shapes=[
            pltpu.VMEM((blocks * LINES, chips * LANES), BF16),
            pltpu.VMEM((blocks // 2 * LANES, chips * LANES), BF16),
        ],
        compiler_params=pltpu.CompilerParams(vmem_limit_bytes=VMEM_LIMIT),
    )(parity, received)


def gate_kernel(side, pair_ref, gain_ref, gate_weight_ref, rows, gate):
    rows[...] = jnp.zeros_like(rows)
    for i in range(side):
        start = (2 * (i % LINES) + i // LINES) * SIDE
        rows[start : start + side, :] = pair_ref[i]
    normed = norm_rows(rows[...], gain_ref[...])
    gate[...] = jax.nn.sigmoid(jnp.dot(normed, gate_weight_ref[...], preferred_element_type=F32))


def gate_rows(pair, gain, gate_weight):
    side, _, channels = pair.shape
    return pl.pallas_call(
        functools.partial(gate_kernel, side),
        out_shape=(
            jax.ShapeDtypeStruct((LINES * LANES, channels), BF16),
            jax.ShapeDtypeStruct((LINES * LANES, channels), F32),
        ),
        compiler_params=pltpu.CompilerParams(vmem_limit_bytes=VMEM_LIMIT),
    )(pair, gain.reshape(1, -1), gate_weight)


def finish_kernel(
    side,
    step,
    rows_ref,
    gate_ref,
    in_ref,
    norm_mid_ref,
    out_weight_ref,
    norm_tr_ref,
    tr_in_ref,
    tr_out_ref,
    out_hbm,
    result,
    out_ref,
    sems,
):
    hidden_width = tr_out_ref.shape[0]
    outgoing = []
    for group in range(LINES // step):
        window = in_ref[:, group * step : (group + 1) * step, :].astype(F32)
        lines = pltpu.einshape("ctl->tcl", window)
        mixed = []
        for u in range(step):
            combined = lines[u]
            average = jnp.mean(combined, axis=0, keepdims=True)
            centered = combined - average
            variance = jnp.mean(centered * centered, axis=0, keepdims=True)
            mixed.append((centered * lax.rsqrt(variance + 1e-05)).T)
        mixed_norm = (jnp.concatenate(mixed, axis=0) * norm_mid_ref[...]).astype(BF16)
        span = slice(group * step * LANES, (group + 1) * step * LANES)
        update = gate_ref[span, :] * jnp.dot(mixed_norm, out_weight_ref[...], preferred_element_type=F32)
        middle = (rows_ref[span, :].astype(F32) + update).astype(BF16)
        tr_normed = norm_rows(middle, norm_tr_ref[...])
        hidden = jnp.dot(tr_normed, tr_in_ref[...], preferred_element_type=F32)
        activated = (jax.nn.silu(hidden[:, :hidden_width]) * hidden[:, hidden_width:]).astype(BF16)
        result[...] = middle.astype(F32) + jnp.dot(activated, tr_out_ref[...], preferred_element_type=F32)
        for half in range(2):
            first = half * LINES + group * step
            count = min(step, side - first)
            for u in range(count):
                start = (2 * u + half) * SIDE
                out_ref[first + u] = result[start : start + side, :].astype(BF16)
            copy = pltpu.make_async_copy(
                out_ref.at[pl.ds(first, count)], out_hbm.at[pl.ds(first, count)], sems.at[len(outgoing)]
            )
            copy.start()
            outgoing.append(copy)
    for copy in outgoing:
        copy.wait()


def finish(shape, rows, gate, received, norm_mid_gain, out_weight, norm_tr_gain, tr_in_weight, tr_out_weight):
    side, _, channels = shape
    step = 16
    return pl.pallas_call(
        functools.partial(finish_kernel, side, step),
        out_shape=jax.ShapeDtypeStruct(shape, BF16),
        out_specs=pl.BlockSpec(memory_space=pltpu.HBM),
        scratch_shapes=[
            pltpu.VMEM((step * LANES, channels), F32),
            pltpu.VMEM(shape, BF16),
            pltpu.SemaphoreType.DMA((2 * LINES // step,)),
        ],
        compiler_params=pltpu.CompilerParams(vmem_limit_bytes=VMEM_LIMIT),
    )(
        rows,
        gate,
        received,
        norm_mid_gain.reshape(1, -1),
        out_weight,
        norm_tr_gain.reshape(1, -1),
        tr_in_weight,
        tr_out_weight,
    )


def local(
    blocks,
    chips,
    pair,
    pair_mask,
    norm_in_gain,
    proj_weight,
    gate_weight,
    norm_mid_gain,
    out_weight,
    norm_tr_gain,
    tr_in_weight,
    tr_out_weight,
):
    every_chip = ("row", "chip")
    core = lax.axis_index("core").astype(jnp.int32).reshape(1)
    sent = project(pair, pair_mask, norm_in_gain, proj_weight)
    received = lax.all_to_all(sent, every_chip, 0, 0, tiled=True)
    rows, gate = gate_rows(pair, norm_in_gain, gate_weight)
    received, rows, gate = lax.optimization_barrier((received, rows, gate))
    other = lax.ppermute(multiply(received, 1 - core, blocks, chips), "core", [(0, 1), (1, 0)])
    keep = multiply(received, core, blocks, chips)
    combined = (keep.astype(F32) + other.astype(F32)).astype(BF16)
    returned = lax.all_to_all(combined, every_chip, 0, 0, tiled=True)
    return finish(
        pair.shape, rows, gate, returned, norm_mid_gain, out_weight, norm_tr_gain, tr_in_weight, tr_out_weight
    )


def solution(mesh):
    blocks, columns = mesh.devices.shape
    chips = columns // 2
    split = Mesh(mesh.devices.reshape(blocks, chips, 2), ("row", "chip", "core"))
    in_specs = (P("row", ("chip", "core"), None), P("row", ("chip", "core"))) + (P(),) * 8
    out_specs = P("row", ("chip", "core"), None)
    return jax.shard_map(
        functools.partial(local, blocks, chips), mesh=split, in_specs=in_specs, out_specs=out_specs, check_vma=False
    )
```

```python
import functools

import jax
import jax.numpy as jnp
from jax import lax
from jax.experimental import pallas as pl
from jax.experimental.pallas import tpu as pltpu
from jax.sharding import Mesh
from jax.sharding import PartitionSpec as P

SIDE = 64
LINES = 32
LANES = 128
VMEM_LIMIT = 48 * 1024 * 1024
F32 = jnp.float32
BF16 = jnp.bfloat16


def norm_rows(values, gain):
    channels = values.shape[-1]
    weight = jnp.full((channels, channels), 1.0 / channels, BF16)
    centered = values.astype(F32) - jnp.dot(values, weight, preferred_element_type=F32)
    variance = jnp.mean(centered * centered, axis=-1, keepdims=True)
    return (centered * lax.rsqrt(variance + 1e-05) * gain).astype(BF16)


def swap_halves(values):
    return pltpu.roll(values, LANES // 2, axis=1)


def low_half(rows):
    return lax.broadcasted_iota(jnp.int32, (rows, LANES), 1) < LANES // 2


def project_kernel(
    side,
    step,
    pair_hbm,
    mask_hbm,
    gain_hbm,
    weight_hbm,
    out_ref,
    pair_ref,
    mask_ref,
    gain_ref,
    weight_ref,
    mask,
    rows,
    sems,
):
    channels = pair_ref.shape[-1]
    groups = LINES // step
    small = [
        pltpu.make_async_copy(source, target, sems.at[n])
        for n, (source, target) in enumerate(((mask_hbm, mask_ref), (weight_hbm, weight_ref), (gain_hbm, gain_ref)))
    ]
    parts = []
    for group in range(groups):
        for half in range(2):
            first = half * LINES + group * step
            span = pl.ds(first, min(step, side - first))
            parts.append(pltpu.make_async_copy(pair_hbm.at[span], pair_ref.at[span], sems.at[3 + len(parts)]))
    for copy in small + parts:
        copy.start()
    rows[...] = jnp.zeros_like(rows)
    mask[...] = jnp.zeros_like(mask)
    for copy in small:
        copy.wait()
    mask[0:side, 0:side] = mask_ref[...].astype(F32)
    low = low_half(LINES)
    keep = jnp.where(low, mask[0:LINES, :], swap_halves(mask[LINES:, :]))
    weight = weight_ref[...].astype(F32).T.astype(BF16)
    for group in range(groups):
        parts[2 * group].wait()
        parts[2 * group + 1].wait()
        for u in range(step):
            for half in range(2):
                i = half * LINES + group * step + u
                if i < side:
                    start = (2 * u + half) * SIDE
                    rows[start : start + side, :] = pair_ref[i]
        sub = 16
        made = ([], [])
        for part in range(step // sub):
            span = slice(part * sub * LANES, (part + 1) * sub * LANES)
            projected = lax.dot_general(
                weight, norm_rows(rows[span, :], gain_ref[...]), (((1,), (1,)), ((), ())), preferred_element_type=F32
            )
            for u in range(sub):
                line = group * step + part * sub + u
                cut = projected[:, u * LANES : (u + 1) * LANES]
                for which in range(2):
                    at = 2 * which * channels
                    gate, value = cut[at : at + channels], cut[at + channels : at + 2 * channels]
                    made[which].append(keep[line : line + 1, :] * jax.nn.sigmoid(gate) * value)
        for which in range(2):
            span = pl.ds(which * LINES + group * step, step)
            out_ref[:, span, :] = pltpu.einshape("tcl->ctl", jnp.stack(made[which])).astype(BF16)


def project(pair, pair_mask, gain, weight):
    side, _, channels = pair.shape
    step = 16
    return pl.pallas_call(
        functools.partial(project_kernel, side, step),
        out_shape=jax.ShapeDtypeStruct((channels, 2 * LINES, LANES), BF16),
        in_specs=[pl.BlockSpec(memory_space=pltpu.HBM)] * 4,
        scratch_shapes=[
            pltpu.VMEM(pair.shape, BF16),
            pltpu.VMEM(pair_mask.shape, jnp.int32),
            pltpu.VMEM((1, channels), F32),
            pltpu.VMEM(weight.shape, BF16),
            pltpu.VMEM((SIDE, LANES), F32),
            pltpu.VMEM((step * LANES, channels), BF16),
            pltpu.SemaphoreType.DMA((3 + 2 * LINES // step,)),
        ],
        compiler_params=pltpu.CompilerParams(vmem_limit_bytes=VMEM_LIMIT),
    )(*(pltpu.with_memory_space_constraint(x, pltpu.HBM) for x in (pair, pair_mask, gain.reshape(1, -1), weight)))


def multiply_kernel(blocks, chips, parity_ref, in_ref, out_ref, left, right):
    parity = parity_ref[0]
    low = low_half(LINES)

    for r in range(blocks):
        for m in range(chips):
            left[r * LINES : (r + 1) * LINES, m * LANES : (m + 1) * LANES] = in_ref[r * chips + m, 0:LINES, :]
    width = 2 * LANES
    for group in range(blocks // 4):
        for s in (2 * group, 2 * group + 1):
            for m in range(chips):
                piece = in_ref[(2 * s + parity) * chips + m, LINES : 2 * LINES, :].astype(F32)
                swapped = swap_halves(piece)
                columns = slice(m * LANES, (m + 1) * LANES)
                for n, values in enumerate(
                    (
                        jnp.where(low, piece, 0.0),
                        jnp.where(low, swapped, 0.0),
                        jnp.where(low, 0.0, swapped),
                        jnp.where(low, 0.0, piece),
                    )
                ):
                    row = s * LANES + n * LINES
                    right[row : row + LINES, columns] = values.astype(BF16)
        product = lax.dot_general(
            left[...],
            right[group * width : (group + 1) * width, :],
            (((1,), (1,)), ((), ())),
            preferred_element_type=F32,
        ).astype(BF16)
        for r in range(blocks):
            for n in range(2):
                out_ref[r * chips + 2 * group + n] = product[
                    r * LINES : (r + 1) * LINES, n * LANES : (n + 1) * LANES
                ]


def multiply(received, parity, blocks, chips):
    return pl.pallas_call(
        functools.partial(multiply_kernel, blocks, chips),
        out_shape=jax.ShapeDtypeStruct((blocks * chips, LINES, LANES), BF16),
        in_specs=[pl.BlockSpec(memory_space=pltpu.SMEM), pl.BlockSpec(memory_space=pltpu.VMEM)],
        scratch_shapes=[
            pltpu.VMEM((blocks * LINES, chips * LANES), BF16),
            pltpu.VMEM((blocks // 2 * LANES, chips * LANES), BF16),
        ],
        compiler_params=pltpu.CompilerParams(vmem_limit_bytes=VMEM_LIMIT),
    )(parity, received)


def gate_kernel(side, pair_ref, gain_ref, gate_weight_ref, rows, gate):
    rows[...] = jnp.zeros_like(rows)
    for i in range(side):
        start = (2 * (i % LINES) + i // LINES) * SIDE
        rows[start : start + side, :] = pair_ref[i]
    normed = norm_rows(rows[...], gain_ref[...])
    gate[...] = jax.nn.sigmoid(jnp.dot(normed, gate_weight_ref[...], preferred_element_type=F32))


def gate_rows(pair, gain, gate_weight):
    side, _, channels = pair.shape
    return pl.pallas_call(
        functools.partial(gate_kernel, side),
        out_shape=(
            jax.ShapeDtypeStruct((LINES * LANES, channels), BF16),
            jax.ShapeDtypeStruct((LINES * LANES, channels), F32),
        ),
        compiler_params=pltpu.CompilerParams(vmem_limit_bytes=VMEM_LIMIT),
    )(pair, gain.reshape(1, -1), gate_weight)


def finish_kernel(
    side,
    step,
    rows_ref,
    gate_ref,
    in_ref,
    norm_mid_ref,
    out_weight_ref,
    norm_tr_ref,
    tr_in_ref,
    tr_out_ref,
    out_hbm,
    out_ref,
    sems,
):
    hidden_width = tr_out_ref.shape[0]
    outgoing = []
    for group in range(LINES // step):
        window = in_ref[:, group * step : (group + 1) * step, :].astype(F32)
        lines = pltpu.einshape("ctl->tcl", window)
        sub = 16
        for part in range(step // sub):
            mixed = []
            for u in range(part * sub, (part + 1) * sub):
                combined = lines[u]
                average = jnp.mean(combined, axis=0, keepdims=True)
                centered = combined - average
                variance = jnp.mean(centered * centered, axis=0, keepdims=True)
                mixed.append((centered * lax.rsqrt(variance + 1e-05)).T)
            mixed_norm = (jnp.concatenate(mixed, axis=0) * norm_mid_ref[...]).astype(BF16)
            begin = (group * step + part * sub) * LANES
            span = slice(begin, begin + sub * LANES)
            update = gate_ref[span, :] * jnp.dot(mixed_norm, out_weight_ref[...], preferred_element_type=F32)
            middle = (rows_ref[span, :].astype(F32) + update).astype(BF16)
            tr_normed = norm_rows(middle, norm_tr_ref[...])
            hidden = jnp.dot(tr_normed, tr_in_ref[...], preferred_element_type=F32)
            activated = (jax.nn.silu(hidden[:, :hidden_width]) * hidden[:, hidden_width:]).astype(BF16)
            made = middle.astype(F32) + jnp.dot(activated, tr_out_ref[...], preferred_element_type=F32)
            for half in range(2):
                first = half * LINES + group * step + part * sub
                count = min(sub, side - first)
                for u in range(count):
                    start = (2 * u + half) * SIDE
                    out_ref[first + u] = made[start : start + side].astype(BF16)
                copy = pltpu.make_async_copy(
                    out_ref.at[pl.ds(first, count)], out_hbm.at[pl.ds(first, count)], sems.at[len(outgoing)]
                )
                copy.start()
                outgoing.append(copy)
    for copy in outgoing:
        copy.wait()


def finish(shape, rows, gate, received, norm_mid_gain, out_weight, norm_tr_gain, tr_in_weight, tr_out_weight):
    side, _, channels = shape
    step = 16
    return pl.pallas_call(
        functools.partial(finish_kernel, side, step),
        out_shape=jax.ShapeDtypeStruct(shape, BF16),
        out_specs=pl.BlockSpec(memory_space=pltpu.HBM),
        scratch_shapes=[
            pltpu.VMEM(shape, BF16),
            pltpu.SemaphoreType.DMA((2 * LINES // 16,)),
        ],
        compiler_params=pltpu.CompilerParams(vmem_limit_bytes=VMEM_LIMIT),
    )(
        rows,
        gate,
        received,
        norm_mid_gain.reshape(1, -1),
        out_weight,
        norm_tr_gain.reshape(1, -1),
        tr_in_weight,
        tr_out_weight,
    )


def local(
    blocks,
    chips,
    pair,
    pair_mask,
    norm_in_gain,
    proj_weight,
    gate_weight,
    norm_mid_gain,
    out_weight,
    norm_tr_gain,
    tr_in_weight,
    tr_out_weight,
):
    every_chip = ("row", "chip")
    core = lax.axis_index("core").astype(jnp.int32).reshape(1)
    sent = project(pair, pair_mask, norm_in_gain, proj_weight)
    sent, core, twin = lax.optimization_barrier((sent, core, 1 - core))
    received = lax.all_to_all(sent, every_chip, 0, 0, tiled=True)
    received, late_pair = lax.optimization_barrier((received, pair))
    other = lax.ppermute(multiply(received, twin, blocks, chips), "core", [(0, 1), (1, 0)])
    keep = multiply(received, core, blocks, chips)
    rows, gate = gate_rows(late_pair, norm_in_gain, gate_weight)
    combined = (keep.astype(F32) + other.astype(F32)).astype(BF16)
    combined, rows, gate = lax.optimization_barrier((combined, rows, gate))
    returned = lax.all_to_all(combined, every_chip, 0, 0, tiled=True)
    return finish(
        pair.shape, rows, gate, returned, norm_mid_gain, out_weight, norm_tr_gain, tr_in_weight, tr_out_weight
    )


def solution(mesh):
    blocks, columns = mesh.devices.shape
    chips = columns // 2
    split = Mesh(mesh.devices.reshape(blocks, chips, 2), ("row", "chip", "core"))
    in_specs = (P("row", ("chip", "core"), None), P("row", ("chip", "core"))) + (P(),) * 8
    out_specs = P("row", ("chip", "core"), None)
    return jax.shard_map(
        functools.partial(local, blocks, chips), mesh=split, in_specs=in_specs, out_specs=out_specs, check_vma=False
    )
```

```python
import functools

import jax
import jax.numpy as jnp
from jax import lax
from jax.experimental import pallas as pl
from jax.experimental.pallas import tpu as pltpu
from jax.sharding import Mesh
from jax.sharding import PartitionSpec as P

SIDE = 64
LINES = 32
LANES = 128
VMEM_LIMIT = 48 * 1024 * 1024
F32 = jnp.float32
BF16 = jnp.bfloat16


def norm_rows(values, gain):
    channels = values.shape[-1]
    weight = jnp.full((channels, channels), 1.0 / channels, BF16)
    centered = values.astype(F32) - jnp.dot(values, weight, preferred_element_type=F32)
    variance = jnp.mean(centered * centered, axis=-1, keepdims=True)
    return (centered * lax.rsqrt(variance + 1e-05) * gain).astype(BF16)


def swap_halves(values):
    return pltpu.roll(values, LANES // 2, axis=1)


def low_half(rows):
    return lax.broadcasted_iota(jnp.int32, (rows, LANES), 1) < LANES // 2


def project_kernel(
    side,
    step,
    pair_hbm,
    mask_hbm,
    gain_hbm,
    weight_hbm,
    out_ref,
    pair_ref,
    mask_ref,
    gain_ref,
    weight_ref,
    mask,
    rows,
    sems,
):
    channels = pair_ref.shape[-1]
    groups = LINES // step
    small = [
        pltpu.make_async_copy(source, target, sems.at[n])
        for n, (source, target) in enumerate(((mask_hbm, mask_ref), (weight_hbm, weight_ref), (gain_hbm, gain_ref)))
    ]
    parts = []
    for group in range(groups):
        for half in range(2):
            first = half * LINES + group * step
            span = pl.ds(first, min(step, side - first))
            parts.append(pltpu.make_async_copy(pair_hbm.at[span], pair_ref.at[span], sems.at[3 + len(parts)]))
    for copy in small + parts:
        copy.start()
    rows[...] = jnp.zeros_like(rows)
    mask[...] = jnp.zeros_like(mask)
    for copy in small:
        copy.wait()
    mask[0:side, 0:side] = mask_ref[...].astype(F32)
    low = low_half(LINES)
    keep = jnp.where(low, mask[0:LINES, :], swap_halves(mask[LINES:, :]))
    weight = weight_ref[...].astype(F32).T.astype(BF16)
    for group in range(groups):
        parts[2 * group].wait()
        parts[2 * group + 1].wait()
        for u in range(step):
            for half in range(2):
                i = half * LINES + group * step + u
                if i < side:
                    start = (2 * u + half) * SIDE
                    rows[start : start + side, :] = pair_ref[i]
        sub = 16
        made = ([], [])
        for part in range(step // sub):
            span = slice(part * sub * LANES, (part + 1) * sub * LANES)
            projected = lax.dot_general(
                weight, norm_rows(rows[span, :], gain_ref[...]), (((1,), (1,)), ((), ())), preferred_element_type=F32
            )
            for u in range(sub):
                line = group * step + part * sub + u
                cut = projected[:, u * LANES : (u + 1) * LANES]
                for which in range(2):
                    at = 2 * which * channels
                    gate, value = cut[at : at + channels], cut[at + channels : at + 2 * channels]
                    made[which].append(keep[line : line + 1, :] * jax.nn.sigmoid(gate) * value)
        for which in range(2):
            span = pl.ds(which * LINES + group * step, step)
            out_ref[:, span, :] = pltpu.einshape("tcl->ctl", jnp.stack(made[which])).astype(BF16)


def project(pair, pair_mask, gain, weight):
    side, _, channels = pair.shape
    step = 16
    return pl.pallas_call(
        functools.partial(project_kernel, side, step),
        out_shape=jax.ShapeDtypeStruct((channels, 2 * LINES, LANES), BF16),
        in_specs=[pl.BlockSpec(memory_space=pltpu.HBM)] * 4,
        scratch_shapes=[
            pltpu.VMEM(pair.shape, BF16),
            pltpu.VMEM(pair_mask.shape, jnp.int32),
            pltpu.VMEM((1, channels), F32),
            pltpu.VMEM(weight.shape, BF16),
            pltpu.VMEM((SIDE, LANES), F32),
            pltpu.VMEM((step * LANES, channels), BF16),
            pltpu.SemaphoreType.DMA((3 + 2 * LINES // step,)),
        ],
        compiler_params=pltpu.CompilerParams(vmem_limit_bytes=VMEM_LIMIT),
    )(*(pltpu.with_memory_space_constraint(x, pltpu.HBM) for x in (pair, pair_mask, gain.reshape(1, -1), weight)))


def multiply_kernel(blocks, chips, parity_ref, in_ref, out_ref, left, right):
    parity = parity_ref[0]
    low = low_half(LINES)

    for r in range(blocks):
        for m in range(chips):
            left[r * LINES : (r + 1) * LINES, m * LANES : (m + 1) * LANES] = in_ref[r * chips + m, 0:LINES, :]
    width = 2 * LANES
    for group in range(blocks // 4):
        for s in (2 * group, 2 * group + 1):
            for m in range(chips):
                piece = in_ref[(2 * s + parity) * chips + m, LINES : 2 * LINES, :].astype(F32)
                swapped = swap_halves(piece)
                columns = slice(m * LANES, (m + 1) * LANES)
                for n, values in enumerate(
                    (
                        jnp.where(low, piece, 0.0),
                        jnp.where(low, swapped, 0.0),
                        jnp.where(low, 0.0, swapped),
                        jnp.where(low, 0.0, piece),
                    )
                ):
                    row = s * LANES + n * LINES
                    right[row : row + LINES, columns] = values.astype(BF16)
        product = lax.dot_general(
            left[...],
            right[group * width : (group + 1) * width, :],
            (((1,), (1,)), ((), ())),
            preferred_element_type=F32,
        ).astype(BF16)
        for r in range(blocks):
            for n in range(2):
                out_ref[r * chips + 2 * group + n] = product[
                    r * LINES : (r + 1) * LINES, n * LANES : (n + 1) * LANES
                ]


def multiply(received, parity, blocks, chips):
    return pl.pallas_call(
        functools.partial(multiply_kernel, blocks, chips),
        out_shape=jax.ShapeDtypeStruct((blocks * chips, LINES, LANES), BF16),
        in_specs=[pl.BlockSpec(memory_space=pltpu.SMEM), pl.BlockSpec(memory_space=pltpu.VMEM)],
        scratch_shapes=[
            pltpu.VMEM((blocks * LINES, chips * LANES), BF16),
            pltpu.VMEM((blocks // 2 * LANES, chips * LANES), BF16),
        ],
        compiler_params=pltpu.CompilerParams(vmem_limit_bytes=VMEM_LIMIT),
    )(parity, received)


def gate_kernel(side, pair_ref, gain_ref, gate_weight_ref, rows, gate):
    rows[...] = jnp.zeros_like(rows)
    for i in range(side):
        start = (2 * (i % LINES) + i // LINES) * SIDE
        rows[start : start + side, :] = pair_ref[i]
    normed = norm_rows(rows[...], gain_ref[...])
    gate[...] = jax.nn.sigmoid(jnp.dot(normed, gate_weight_ref[...], preferred_element_type=F32))


def keep_kernel(blocks, chips, side, parity_ref, in_ref, pair_ref, gain_ref, gate_ref, out_ref, rows, gate, left, right):
    gate_kernel(side, pair_ref, gain_ref, gate_ref, rows, gate)
    multiply_kernel(blocks, chips, parity_ref, in_ref, out_ref, left, right)


def multiply_and_gate(received, parity, blocks, chips, pair, gain, gate_weight):
    side, _, channels = pair.shape
    return pl.pallas_call(
        functools.partial(keep_kernel, blocks, chips, side),
        out_shape=(
            jax.ShapeDtypeStruct((blocks * chips, LINES, LANES), BF16),
            jax.ShapeDtypeStruct((LINES * LANES, channels), BF16),
            jax.ShapeDtypeStruct((LINES * LANES, channels), F32),
        ),
        in_specs=[pl.BlockSpec(memory_space=pltpu.SMEM)] + [pl.BlockSpec(memory_space=pltpu.VMEM)] * 4,
        scratch_shapes=[
            pltpu.VMEM((blocks * LINES, chips * LANES), BF16),
            pltpu.VMEM((blocks // 2 * LANES, chips * LANES), BF16),
        ],
        compiler_params=pltpu.CompilerParams(vmem_limit_bytes=VMEM_LIMIT // 2),
    )(parity, received, pair, gain.reshape(1, -1), gate_weight)


def finish_kernel(
    side,
    step,
    rows_ref,
    gate_ref,
    in_ref,
    norm_mid_ref,
    out_weight_ref,
    norm_tr_ref,
    tr_in_ref,
    tr_out_ref,
    out_hbm,
    out_ref,
    sems,
):
    hidden_width = tr_out_ref.shape[0]
    outgoing = []
    for group in range(LINES // step):
        window = in_ref[:, group * step : (group + 1) * step, :].astype(F32)
        lines = pltpu.einshape("ctl->tcl", window)
        sub = 16
        for part in range(step // sub):
            mixed = []
            for u in range(part * sub, (part + 1) * sub):
                combined = lines[u]
                average = jnp.mean(combined, axis=0, keepdims=True)
                centered = combined - average
                variance = jnp.mean(centered * centered, axis=0, keepdims=True)
                mixed.append((centered * lax.rsqrt(variance + 1e-05)).T)
            mixed_norm = (jnp.concatenate(mixed, axis=0) * norm_mid_ref[...]).astype(BF16)
            begin = (group * step + part * sub) * LANES
            span = slice(begin, begin + sub * LANES)
            update = gate_ref[span, :] * jnp.dot(mixed_norm, out_weight_ref[...], preferred_element_type=F32)
            middle = (rows_ref[span, :].astype(F32) + update).astype(BF16)
            tr_normed = norm_rows(middle, norm_tr_ref[...])
            hidden = jnp.dot(tr_normed, tr_in_ref[...], preferred_element_type=F32)
            activated = (jax.nn.silu(hidden[:, :hidden_width]) * hidden[:, hidden_width:]).astype(BF16)
            made = middle.astype(F32) + jnp.dot(activated, tr_out_ref[...], preferred_element_type=F32)
            for half in range(2):
                first = half * LINES + group * step + part * sub
                count = min(sub, side - first)
                for u in range(count):
                    start = (2 * u + half) * SIDE
                    out_ref[first + u] = made[start : start + side].astype(BF16)
                copy = pltpu.make_async_copy(
                    out_ref.at[pl.ds(first, count)], out_hbm.at[pl.ds(first, count)], sems.at[len(outgoing)]
                )
                copy.start()
                outgoing.append(copy)
    for copy in outgoing:
        copy.wait()


def finish(shape, rows, gate, received, norm_mid_gain, out_weight, norm_tr_gain, tr_in_weight, tr_out_weight):
    side, _, channels = shape
    step = 16
    return pl.pallas_call(
        functools.partial(finish_kernel, side, step),
        out_shape=jax.ShapeDtypeStruct(shape, BF16),
        out_specs=pl.BlockSpec(memory_space=pltpu.HBM),
        scratch_shapes=[
            pltpu.VMEM(shape, BF16),
            pltpu.SemaphoreType.DMA((2 * LINES // 16,)),
        ],
        compiler_params=pltpu.CompilerParams(vmem_limit_bytes=VMEM_LIMIT),
    )(
        rows,
        gate,
        received,
        norm_mid_gain.reshape(1, -1),
        out_weight,
        norm_tr_gain.reshape(1, -1),
        tr_in_weight,
        tr_out_weight,
    )


def local(
    blocks,
    chips,
    pair,
    pair_mask,
    norm_in_gain,
    proj_weight,
    gate_weight,
    norm_mid_gain,
    out_weight,
    norm_tr_gain,
    tr_in_weight,
    tr_out_weight,
):
    every_chip = ("row", "chip")
    core = lax.axis_index("core").astype(jnp.int32).reshape(1)
    sent = project(pair, pair_mask, norm_in_gain, proj_weight)
    sent, core, twin = lax.optimization_barrier((sent, core, 1 - core))
    received = lax.all_to_all(sent, every_chip, 0, 0, tiled=True)
    other = lax.ppermute(multiply(received, twin, blocks, chips), "core", [(0, 1), (1, 0)])
    keep, rows, gate = multiply_and_gate(received, core, blocks, chips, pair, norm_in_gain, gate_weight)
    combined = (keep.astype(F32) + other.astype(F32)).astype(BF16)
    combined, rows, gate = lax.optimization_barrier((combined, rows, gate))
    returned = lax.all_to_all(combined, every_chip, 0, 0, tiled=True)
    return finish(
        pair.shape, rows, gate, returned, norm_mid_gain, out_weight, norm_tr_gain, tr_in_weight, tr_out_weight
    )


def solution(mesh):
    blocks, columns = mesh.devices.shape
    chips = columns // 2
    split = Mesh(mesh.devices.reshape(blocks, chips, 2), ("row", "chip", "core"))
    in_specs = (P("row", ("chip", "core"), None), P("row", ("chip", "core"))) + (P(),) * 8
    out_specs = P("row", ("chip", "core"), None)
    return jax.shard_map(
        functools.partial(local, blocks, chips), mesh=split, in_specs=in_specs, out_specs=out_specs, check_vma=False
    )
```

```python
import functools

import jax
import jax.numpy as jnp
from jax import lax
from jax.experimental import pallas as pl
from jax.experimental.pallas import tpu as pltpu
from jax.sharding import Mesh
from jax.sharding import PartitionSpec as P

SIDE = 64
LINES = 32
LANES = 128
VMEM_LIMIT = 48 * 1024 * 1024
F32 = jnp.float32
BF16 = jnp.bfloat16


def norm_rows(values, gain):
    channels = values.shape[-1]
    weight = jnp.full((channels, channels), 1.0 / channels, BF16)
    centered = values.astype(F32) - jnp.dot(values, weight, preferred_element_type=F32)
    variance = jnp.mean(centered * centered, axis=-1, keepdims=True)
    return (centered * lax.rsqrt(variance + 1e-05) * gain).astype(BF16)


def swap_halves(values):
    return pltpu.roll(values, LANES // 2, axis=1)


def low_half(rows):
    return lax.broadcasted_iota(jnp.int32, (rows, LANES), 1) < LANES // 2


def project_kernel(
    side,
    step,
    pair_hbm,
    mask_hbm,
    gain_hbm,
    weight_hbm,
    out_ref,
    pair_ref,
    mask_ref,
    gain_ref,
    weight_ref,
    mask,
    rows,
    sems,
):
    channels = pair_ref.shape[-1]
    groups = LINES // step
    small = [
        pltpu.make_async_copy(source, target, sems.at[n])
        for n, (source, target) in enumerate(((mask_hbm, mask_ref), (weight_hbm, weight_ref), (gain_hbm, gain_ref)))
    ]
    parts = []
    for group in range(groups):
        for half in range(2):
            first = half * LINES + group * step
            span = pl.ds(first, min(step, side - first))
            parts.append(pltpu.make_async_copy(pair_hbm.at[span], pair_ref.at[span], sems.at[3 + len(parts)]))
    for copy in small + parts:
        copy.start()
    rows[...] = jnp.zeros_like(rows)
    mask[...] = jnp.zeros_like(mask)
    for copy in small:
        copy.wait()
    mask[0:side, 0:side] = mask_ref[...].astype(F32)
    low = low_half(LINES)
    keep = jnp.where(low, mask[0:LINES, :], swap_halves(mask[LINES:, :]))
    weight = weight_ref[...].astype(F32).T.astype(BF16)
    for group in range(groups):
        parts[2 * group].wait()
        parts[2 * group + 1].wait()
        for u in range(step):
            for half in range(2):
                i = half * LINES + group * step + u
                if i < side:
                    start = (2 * u + half) * SIDE
                    rows[start : start + side, :] = pair_ref[i]
        sub = 16
        made = ([], [])
        for part in range(step // sub):
            span = slice(part * sub * LANES, (part + 1) * sub * LANES)
            projected = lax.dot_general(
                weight, norm_rows(rows[span, :], gain_ref[...]), (((1,), (1,)), ((), ())), preferred_element_type=F32
            )
            for u in range(sub):
                line = group * step + part * sub + u
                cut = projected[:, u * LANES : (u + 1) * LANES]
                for which in range(2):
                    at = 2 * which * channels
                    gate, value = cut[at : at + channels], cut[at + channels : at + 2 * channels]
                    made[which].append(keep[line : line + 1, :] * jax.nn.sigmoid(gate) * value)
        for which in range(2):
            span = pl.ds(which * LINES + group * step, step)
            out_ref[:, span, :] = pltpu.einshape("tcl->ctl", jnp.stack(made[which])).astype(BF16)


def project(pair, pair_mask, gain, weight):
    side, _, channels = pair.shape
    step = 16
    return pl.pallas_call(
        functools.partial(project_kernel, side, step),
        out_shape=jax.ShapeDtypeStruct((channels, 2 * LINES, LANES), BF16),
        in_specs=[pl.BlockSpec(memory_space=pltpu.HBM)] * 4,
        scratch_shapes=[
            pltpu.VMEM(pair.shape, BF16),
            pltpu.VMEM(pair_mask.shape, jnp.int32),
            pltpu.VMEM((1, channels), F32),
            pltpu.VMEM(weight.shape, BF16),
            pltpu.VMEM((SIDE, LANES), F32),
            pltpu.VMEM((step * LANES, channels), BF16),
            pltpu.SemaphoreType.DMA((3 + 2 * LINES // step,)),
        ],
        compiler_params=pltpu.CompilerParams(vmem_limit_bytes=VMEM_LIMIT),
    )(*(pltpu.with_memory_space_constraint(x, pltpu.HBM) for x in (pair, pair_mask, gain.reshape(1, -1), weight)))


def multiply_kernel(blocks, chips, parity_ref, in_ref, out_ref, left, right):
    parity = parity_ref[0]
    low = low_half(LINES)

    for r in range(blocks):
        for m in range(chips):
            left[r * LINES : (r + 1) * LINES, m * LANES : (m + 1) * LANES] = in_ref[r * chips + m, 0:LINES, :]
    width = 2 * LANES
    for group in range(blocks // 4):
        for s in (2 * group, 2 * group + 1):
            for m in range(chips):
                piece = in_ref[(2 * s + parity) * chips + m, LINES : 2 * LINES, :].astype(F32)
                swapped = swap_halves(piece)
                columns = slice(m * LANES, (m + 1) * LANES)
                for n, values in enumerate(
                    (
                        jnp.where(low, piece, 0.0),
                        jnp.where(low, swapped, 0.0),
                        jnp.where(low, 0.0, swapped),
                        jnp.where(low, 0.0, piece),
                    )
                ):
                    row = s * LANES + n * LINES
                    right[row : row + LINES, columns] = values.astype(BF16)
        product = lax.dot_general(
            left[...],
            right[group * width : (group + 1) * width, :],
            (((1,), (1,)), ((), ())),
            preferred_element_type=F32,
        ).astype(BF16)
        for r in range(blocks):
            for n in range(2):
                out_ref[r * chips + 2 * group + n] = product[
                    r * LINES : (r + 1) * LINES, n * LANES : (n + 1) * LANES
                ]


def multiply(received, parity, blocks, chips):
    return pl.pallas_call(
        functools.partial(multiply_kernel, blocks, chips),
        out_shape=jax.ShapeDtypeStruct((blocks * chips, LINES, LANES), BF16),
        in_specs=[pl.BlockSpec(memory_space=pltpu.SMEM), pl.BlockSpec(memory_space=pltpu.VMEM)],
        scratch_shapes=[
            pltpu.VMEM((blocks * LINES, chips * LANES), BF16),
            pltpu.VMEM((blocks // 2 * LANES, chips * LANES), BF16),
        ],
        compiler_params=pltpu.CompilerParams(vmem_limit_bytes=VMEM_LIMIT),
    )(parity, received)


def gate_kernel(side, pair_ref, gain_ref, gate_weight_ref, rows, gate):
    rows[...] = jnp.zeros_like(rows)
    for i in range(side):
        start = (2 * (i % LINES) + i // LINES) * SIDE
        rows[start : start + side, :] = pair_ref[i]
    normed = norm_rows(rows[...], gain_ref[...])
    gate[...] = jax.nn.sigmoid(jnp.dot(normed, gate_weight_ref[...], preferred_element_type=F32))


def keep_kernel(blocks, chips, side, parity_ref, in_ref, pair_ref, gain_ref, gate_ref, out_ref, rows, gate, left, right):
    gate_kernel(side, pair_ref, gain_ref, gate_ref, rows, gate)
    multiply_kernel(blocks, chips, parity_ref, in_ref, out_ref, left, right)


def multiply_and_gate(received, parity, blocks, chips, pair, gain, gate_weight):
    side, _, channels = pair.shape
    return pl.pallas_call(
        functools.partial(keep_kernel, blocks, chips, side),
        out_shape=(
            jax.ShapeDtypeStruct((blocks * chips, LINES, LANES), BF16),
            jax.ShapeDtypeStruct((LINES * LANES, channels), BF16),
            jax.ShapeDtypeStruct((LINES * LANES, channels), F32),
        ),
        in_specs=[pl.BlockSpec(memory_space=pltpu.SMEM)] + [pl.BlockSpec(memory_space=pltpu.VMEM)] * 4,
        scratch_shapes=[
            pltpu.VMEM((blocks * LINES, chips * LANES), BF16),
            pltpu.VMEM((blocks // 2 * LANES, chips * LANES), BF16),
        ],
        compiler_params=pltpu.CompilerParams(vmem_limit_bytes=VMEM_LIMIT // 2),
    )(parity, received, pair, gain.reshape(1, -1), gate_weight)


def finish_kernel(
    side,
    step,
    rows_ref,
    gate_ref,
    in_ref,
    norm_mid_ref,
    out_weight_ref,
    norm_tr_ref,
    tr_in_ref,
    tr_out_ref,
    out_hbm,
    out_ref,
    sems,
):
    hidden_width = tr_out_ref.shape[0]
    outgoing = []
    lines = []
    for group in range(LINES // step):
        window = in_ref[:, group * step : (group + 1) * step, :].astype(F32)
        block = pltpu.einshape("ctl->tcl", window)
        lines += [block[u] for u in range(step)]
    begin = 0
    for count_lines in (24, 8):
        mixed = []
        for combined in lines[begin : begin + count_lines]:
            average = jnp.mean(combined, axis=0, keepdims=True)
            centered = combined - average
            variance = jnp.mean(centered * centered, axis=0, keepdims=True)
            mixed.append((centered * lax.rsqrt(variance + 1e-05)).T)
        mixed_norm = (jnp.concatenate(mixed, axis=0) * norm_mid_ref[...]).astype(BF16)
        span = slice(begin * LANES, (begin + count_lines) * LANES)
        update = gate_ref[span, :] * jnp.dot(mixed_norm, out_weight_ref[...], preferred_element_type=F32)
        middle = (rows_ref[span, :].astype(F32) + update).astype(BF16)
        tr_normed = norm_rows(middle, norm_tr_ref[...])
        hidden = jnp.dot(tr_normed, tr_in_ref[...], preferred_element_type=F32)
        activated = (jax.nn.silu(hidden[:, :hidden_width]) * hidden[:, hidden_width:]).astype(BF16)
        made = middle.astype(F32) + jnp.dot(activated, tr_out_ref[...], preferred_element_type=F32)
        for half in range(2):
            first = half * LINES + begin
            count = min(count_lines, side - first)
            for u in range(count):
                start = (2 * u + half) * SIDE
                out_ref[first + u] = made[start : start + side].astype(BF16)
            copy = pltpu.make_async_copy(
                out_ref.at[pl.ds(first, count)], out_hbm.at[pl.ds(first, count)], sems.at[len(outgoing)]
            )
            copy.start()
            outgoing.append(copy)
        begin += count_lines
    for copy in outgoing:
        copy.wait()


def finish(shape, rows, gate, received, norm_mid_gain, out_weight, norm_tr_gain, tr_in_weight, tr_out_weight):
    side, _, channels = shape
    step = 16
    return pl.pallas_call(
        functools.partial(finish_kernel, side, step),
        out_shape=jax.ShapeDtypeStruct(shape, BF16),
        out_specs=pl.BlockSpec(memory_space=pltpu.HBM),
        scratch_shapes=[
            pltpu.VMEM(shape, BF16),
            pltpu.SemaphoreType.DMA((2 * LINES // 16,)),
        ],
        compiler_params=pltpu.CompilerParams(vmem_limit_bytes=VMEM_LIMIT),
    )(
        rows,
        gate,
        received,
        norm_mid_gain.reshape(1, -1),
        out_weight,
        norm_tr_gain.reshape(1, -1),
        tr_in_weight,
        tr_out_weight,
    )


def local(
    blocks,
    chips,
    pair,
    pair_mask,
    norm_in_gain,
    proj_weight,
    gate_weight,
    norm_mid_gain,
    out_weight,
    norm_tr_gain,
    tr_in_weight,
    tr_out_weight,
):
    every_chip = ("row", "chip")
    core = lax.axis_index("core").astype(jnp.int32).reshape(1)
    sent = project(pair, pair_mask, norm_in_gain, proj_weight)
    sent, core, twin = lax.optimization_barrier((sent, core, 1 - core))
    received = lax.all_to_all(sent, every_chip, 0, 0, tiled=True)
    other = lax.ppermute(multiply(received, twin, blocks, chips), "core", [(0, 1), (1, 0)])
    keep, rows, gate = multiply_and_gate(received, core, blocks, chips, pair, norm_in_gain, gate_weight)
    combined = (keep.astype(F32) + other.astype(F32)).astype(BF16)
    combined, rows, gate = lax.optimization_barrier((combined, rows, gate))
    returned = lax.all_to_all(combined, every_chip, 0, 0, tiled=True)
    return finish(
        pair.shape, rows, gate, returned, norm_mid_gain, out_weight, norm_tr_gain, tr_in_weight, tr_out_weight
    )


def solution(mesh):
    blocks, columns = mesh.devices.shape
    chips = columns // 2
    split = Mesh(mesh.devices.reshape(blocks, chips, 2), ("row", "chip", "core"))
    in_specs = (P("row", ("chip", "core"), None), P("row", ("chip", "core"))) + (P(),) * 8
    out_specs = P("row", ("chip", "core"), None)
    return jax.shard_map(
        functools.partial(local, blocks, chips), mesh=split, in_specs=in_specs, out_specs=out_specs, check_vma=False
    )
```
